32 devices in a mesh: dp: 8 (over y, x, core), ctx: 4 (over z).
Axes of the slice: x: 2, y: 2, z: 4, core: 2. Of those that a mesh axis runs over, the one named last changes fastest.
Arguments:
- tokens: bfloat16 [16, 1536, 960], P('dp', 'ctx'), may hold values from -6 to 6
- lengths: int32 [16, 3], P('dp'), may hold values from 1 to 1534, as said below
- gain_attn: bfloat16 [960], P('dp'), may hold values from 0.5 to 1.5
- w_query: bfloat16 [960, 960], P('dp'), may hold values from -0.1875 to 0.1875
- w_key: bfloat16 [960, 320], P('dp'), may hold values from -0.1875 to 0.1875
- w_value: bfloat16 [960, 320], P('dp'), may hold values from -0.1875 to 0.1875
- w_out: bfloat16 [960, 960], P(None, 'dp'), may hold values from -3.5 to 3.5
- gain_ffn: bfloat16 [960], P('dp'), may hold values from 0.5 to 1.5
- w_gate: bfloat16 [960, 2560], P('dp'), may hold values from -0.1875 to 0.1875
- w_up: bfloat16 [960, 2560], P('dp'), may hold values from -0.1875 to 0.1875
- w_down: bfloat16 [2560, 960], P(None, 'dp'), may hold values from -0.125 to 0.125
- cotangent: bfloat16 [16, 1536, 960], P('dp', 'ctx'), may hold values from -6 to 6
Outputs:
- output: bfloat16 [16, 1536, 960], P('dp', 'ctx')
- d_tokens: bfloat16 [16, 1536, 960], P('dp', 'ctx')
- grad_gain_attn: float32 [960], P('dp')
- grad_w_query: float32 [960, 960], P('dp')
- grad_w_key: float32 [960, 320], P('dp')
- grad_w_value: float32 [960, 320], P('dp')
- grad_w_out: float32 [960, 960], P(None, 'dp')
- grad_gain_ffn: float32 [960], P('dp')
- grad_w_gate: float32 [960, 2560], P('dp')
- grad_w_up: float32 [960, 2560], P('dp')
- grad_w_down: float32 [2560, 960], P(None, 'dp')
The draws below stay inside these ranges and needn't reach their ends.
Inputs may be any that keep to these rules, and one draw needn't show every extreme that they name: Each row holds three document lengths summing to 1536; the first and the last are at most 96; in one row the first and the last are 1.
All inputs are finite; a program needn't handle non-finite values.
Results may differ from the reference program's by a relative error of at most 0.02.
Values may be sent and summed in bfloat16 or wider, within the bound.
A program may use at most 256 MiB of HBM per device.

```python
import math
import jax
import jax.numpy as jnp
from jax import lax

D = 960
H = 15
KVH = 5
HD = 64
FF = 2560
TOK_MB = 384
PACK = 1536
BATCH = 16
QW = 960
KW = 320


def draw_lengths(key, part):
    key = jax.random.fold_in(key, 7)
    lead_key, trail_key, pick_key = jax.random.split(key, 3)
    leading = jax.random.randint(lead_key, (BATCH,), 1, TOK_MB // 4 + 1)
    trailing = jax.random.randint(trail_key, (BATCH,), 1, TOK_MB // 4 + 1)
    chosen = jax.random.randint(pick_key, (), 0, BATCH)
    marked = jnp.arange(BATCH) == chosen
    leading = jnp.where(marked, 1, leading)
    trailing = jnp.where(marked, 1, trailing)
    middle_len = PACK - leading - trailing
    return jnp.stack([leading, middle_len, trailing], axis=1).astype(jnp.int32)


def level_of(rng, shape, cuts, least, top_value):
    def one(position, shards_of):
        steps = jax.random.uniform(jax.random.fold_in(jax.random.fold_in(rng, 6), position), (shards_of,), jnp.float32, least / len(cuts), top_value / len(cuts))
        return jnp.repeat(jnp.exp(steps), shape[position] // shards_of).reshape((-1,) + (1,) * (len(shape) - position - 1))

    factor_of = one(*cuts[0])
    for cut in cuts[1:]:
        factor_of = factor_of * one(*cut)
    return factor_of


def normal_values(rng, dims, deviation, most, shards=(), held_as=jnp.bfloat16):
    gain = level_of(rng, dims, shards, -0.22, 0.18) if shards else 1.0
    array = jax.random.normal(rng, dims, jnp.float32) * deviation * gain
    return jnp.minimum(jnp.maximum(array, -most), most).astype(held_as)


def setup_inputs(seed: int = 0) -> dict:
    keys = jax.random.split(jax.random.key(seed), 13)
    tokens = normal_values(keys[0], (BATCH, PACK, D), 1.0, 6.0, ((0, 8), (1, 4)))
    lengths = draw_lengths(jax.random.fold_in(keys[12], 71), 0)
    gain_attn = jnp.clip(1.0 + 0.1 * jax.random.normal(keys[2], (D,), jnp.float32), 0.5, 1.5).astype(jnp.bfloat16)
    w_query = normal_values(keys[3], (D, QW), D ** -0.5, 0.1875, ((0, 8),))
    w_key = normal_values(keys[4], (D, KW), D ** -0.5, 0.1875, ((0, 8),))
    w_value = normal_values(keys[5], (D, KW), D ** -0.5, 0.1875, ((0, 8),))
    w_out = normal_values(keys[6], (QW, D), (max(H * HD // 256, 1)) ** -0.5, 3.5, ((1, 8),))
    gain_ffn = jnp.clip(1.0 + 0.1 * jax.random.normal(keys[7], (D,), jnp.float32), 0.5, 1.5).astype(jnp.bfloat16)
    w_gate = normal_values(keys[8], (D, FF), D ** -0.5, 0.1875, ((0, 8),))
    w_up = normal_values(keys[9], (D, FF), D ** -0.5, 0.1875, ((0, 8),))
    w_down = normal_values(keys[10], (FF, D), FF ** -0.5, 0.125, ((1, 8),))
    cotangent = normal_values(keys[11], (BATCH, PACK, D), 1.0, 6.0, ((0, 8), (1, 4)))
    return dict(tokens=tokens, lengths=lengths, gain_attn=gain_attn, w_query=w_query, w_key=w_key, w_value=w_value, w_out=w_out, gain_ffn=gain_ffn, w_gate=w_gate, w_up=w_up, w_down=w_down, cotangent=cotangent)


NORM_EPSILON = 1e-05
ROPE_BASE = 10000.0
MASKED_SCORE = -1e+30

@jax.custom_vjp
def low(v):
    return lax.optimization_barrier(v.astype(jnp.bfloat16)).astype(jnp.float32)

@jax.custom_vjp
def low_back(v):
    return v

def low_keep(v):
    return (low(v), None)

def low_pass(kept, grad):
    return (grad,)

def back_keep(v):
    return (v, None)

def back_low(kept, grad):
    return (low(grad),)
low.defvjp(low_keep, low_pass)
low_back.defvjp(back_keep, back_low)

def norm_apply(values, gain_vec):
    return values * lax.rsqrt(lax.optimization_barrier(jnp.mean(values * values, -1, keepdims=True)) + NORM_EPSILON) * gain_vec

def rotate(values, positions):
    half_width = values.shape[-1] // 2
    frequency = ROPE_BASE ** (-jnp.arange(half_width, dtype=jnp.float32) / half_width)
    angles = positions.astype(jnp.float32)[:, None] * frequency[None, :]
    cosine = jnp.cos(angles)[:, None, :]
    sine_vals = jnp.sin(angles)[:, None, :]
    first_half = values[..., :half_width]
    second_half = values[..., half_width:]
    return jnp.concatenate([first_half * cosine - second_half * sine_vals, second_half * cosine + first_half * sine_vals], -1)

def doc_layout(doc_lengths, places):
    first_end = doc_lengths[0]
    second_end = doc_lengths[0] + doc_lengths[1]
    after_first = (places >= first_end).astype(jnp.int32)
    after_second = (places >= second_end).astype(jnp.int32)
    return (after_first + after_second, places - after_first * first_end - after_second * doc_lengths[1])

def block_forward(stream, weight_set, doc_ids, positions):
    gain_attn, w_query, w_key, w_value, w_out, gain_ffn, w_gate, w_up, w_down = weight_set
    tok_rows = stream.shape[0]
    groups = H // KVH
    highest = lax.Precision.HIGHEST
    score_scale = 1.0 / math.sqrt(HD)
    normed = low(norm_apply(stream, gain_attn))
    query_lin = low_back(jnp.dot(normed, w_query, precision=highest))
    key_lin = low_back(jnp.dot(normed, w_key, precision=highest))
    value_rows = low(low_back(jnp.dot(normed, w_value, precision=highest))).reshape(tok_rows, KVH, HD)
    queries = low(rotate(query_lin.reshape(tok_rows, H, HD), positions)).reshape(tok_rows, KVH, groups, HD)
    key_rows = low(rotate(key_lin.reshape(tok_rows, KVH, HD), positions))
    block_rows = min(tok_rows, 512)
    block_count = tok_rows // block_rows

    def attend(query_block):
        query_part, doc_part, pos_part = query_block
        scores = low_back(jnp.einsum('nkgd,ckd->kgnc', query_part, key_rows, precision=highest) * score_scale)
        allowed = (doc_ids[None, :] == doc_part[:, None]) & (positions[None, :] <= pos_part[:, None])
        scores = jnp.where(allowed, scores, MASKED_SCORE)
        prob_low = low(jax.nn.softmax(scores, axis=-1))
        return jnp.einsum('kgnc,ckd->nkgd', prob_low, value_rows, precision=highest)
    attended = lax.map(jax.checkpoint(attend), (queries.reshape(block_count, block_rows, KVH, groups, HD), doc_ids.reshape(block_count, block_rows), positions.reshape(block_count, block_rows)))
    attn_low = low(low_back(attended.reshape(tok_rows, H * HD)))
    middle = stream + low_back(jnp.dot(attn_low, w_out, precision=highest))
    normed_two = low(norm_apply(middle, gain_ffn))
    gate_lin = low_back(jnp.dot(normed_two, w_gate, precision=highest))
    up_lin = low_back(jnp.dot(normed_two, w_up, precision=highest))
    hidden = low(jax.nn.silu(gate_lin) * up_lin)
    return middle + low_back(jnp.dot(hidden, w_down, precision=highest))

def reference(tokens, lengths, gain_attn, w_query, w_key, w_value, w_out, gain_ffn, w_gate, w_up, w_down, cotangent):
    weight_set = tuple((weight_arg.astype(jnp.float32) for weight_arg in (gain_attn, w_query, w_key, w_value, w_out, gain_ffn, w_gate, w_up, w_down)))
    places = jnp.arange(tokens.shape[1], dtype=jnp.int32)

    def one_pack(totals, packed):
        pack_tokens, doc_lengths, pack_cot = packed
        doc_ids, positions = doc_layout(doc_lengths, places)

        def forward(stream, weights_in):
            return block_forward(stream, weights_in, doc_ids, positions)
        result, pullback = jax.vjp(forward, pack_tokens.astype(jnp.float32), weight_set)
        d_stream, d_weights = pullback(pack_cot.astype(jnp.float32))
        totals = tuple((before_sum + term for before_sum, term in zip(totals, d_weights)))
        return (totals, (result.astype(jnp.bfloat16), d_stream.astype(jnp.bfloat16)))
    zero_grads = tuple((jnp.zeros(weight_arg.shape, jnp.float32) for weight_arg in weight_set))
    totals, (outputs, d_tokens) = lax.scan(one_pack, zero_grads, (tokens, lengths, cotangent))
    return (outputs, d_tokens, totals[0], totals[1], totals[2], totals[3], totals[4], totals[5], totals[6], totals[7], totals[8])
```

```python
import functools
import math

import jax
import jax.numpy as jnp
from jax import lax
from jax.experimental import pallas as pl
from jax.experimental.pallas import tpu as pltpu
from jax.sharding import PartitionSpec as P

D = 960
H = 15
KVH = 5
HD = 64
FF = 2560
GROUPS = H // KVH
QW = H * HD
KW = KVH * HD

NORM_EPSILON = 1e-05
ROPE_BASE = 10000.0
MASKED_SCORE = -1e30
F32 = jnp.float32
BF16 = jnp.bfloat16


def dot(left, right, dims):
    return lax.dot_general(left, right, (dims, ((), ())), preferred_element_type=F32)


def fill_bias(info_ref, bias, tok):
    pack = pl.program_id(0)
    own = info_ref[pack, 0]
    first_end = info_ref[pack, 1]
    second_end = info_ref[pack, 2]
    query = own * tok + lax.broadcasted_iota(jnp.int32, (tok, tok), 1)
    start = jnp.where(
        query >= second_end, second_end, jnp.where(query >= first_end, first_end, 0)
    )

    def one(block, carry):
        key = block * tok + lax.broadcasted_iota(jnp.int32, (tok, tok), 0)
        allowed = (key >= start) & (key <= query)
        bias[block] = jnp.where(allowed, 0.0, MASKED_SCORE)
        return carry

    lax.fori_loop(0, own + 1, one, 0)


def forward_kernel(tok, info_ref, q_ref, kv_ref, attn_ref, lse_ref, bias):
    own = info_ref[pl.program_id(0), 0]

    @pl.when(pl.program_id(1) == 0)
    def _():
        fill_bias(info_ref, bias, tok)

    def one(step, carry):
        block = own - step
        keys = kv_ref[block, 0].T
        values = kv_ref[block, 1]
        mask = bias[block]
        state = []
        for g in range(GROUPS):
            top, total, accum = carry[g]
            scores = dot(keys, q_ref[g * HD : (g + 1) * HD, :], ((1,), (0,))) + mask
            new_top = jnp.maximum(top, jnp.max(scores, 0, keepdims=True))
            scaled = jnp.exp(top - new_top)
            expos = jnp.exp(scores - new_top)
            total = total * scaled + jnp.sum(expos, 0, keepdims=True)
            accum = accum * scaled + dot(values, expos.astype(BF16), ((1,), (0,)))
            state.append((new_top, total, accum))
        return tuple(state)

    begin = tuple(
        (
            jnp.full((1, tok), MASKED_SCORE, F32),
            jnp.zeros((1, tok), F32),
            jnp.zeros((HD, tok), F32),
        )
        for _ in range(GROUPS)
    )
    final = lax.fori_loop(0, own + 1, one, begin)
    for g in range(GROUPS):
        top, total, accum = final[g]
        attn_ref[g * HD : (g + 1) * HD, :] = (accum / total).astype(BF16)
        lse_ref[0, g : g + 1, :] = top + jnp.log(total)


def backward_kernel(
    tok, count, info_ref, q_ref, kv_ref, do_ref, attn_ref, lse_ref, dq_ref, dkv_ref, bias
):
    own = info_ref[pl.program_id(0), 0]

    @pl.when(pl.program_id(1) == 0)
    def _():
        fill_bias(info_ref, bias, tok)

    dq_ref[...] = jnp.zeros_like(dq_ref)
    queries = [q_ref[g * HD : (g + 1) * HD, :] for g in range(GROUPS)]
    d_attn = [do_ref[g * HD : (g + 1) * HD, :] for g in range(GROUPS)]
    queries_t = [value.T for value in queries]
    d_attn_t = [value.T for value in d_attn]
    delta = [
        jnp.sum(
            d_attn[g].astype(F32) * attn_ref[g * HD : (g + 1) * HD, :].astype(F32),
            0,
            keepdims=True,
        )
        for g in range(GROUPS)
    ]

    def one(block, carry):
        keys = kv_ref[block, 0]
        keys_t = keys.T
        values_t = kv_ref[block, 1].T
        mask = bias[block]
        dk = jnp.zeros((tok, HD), F32)
        dv = jnp.zeros((tok, HD), F32)
        for g in range(GROUPS):
            scores = dot(keys_t, queries[g], ((1,), (0,))) + mask
            probs = jnp.exp(scores - lse_ref[0, g : g + 1, :])
            d_probs = dot(values_t, d_attn[g], ((1,), (0,)))
            d_scores = (probs * (d_probs - delta[g])).astype(BF16)
            dv = dv + dot(probs.astype(BF16), d_attn_t[g], ((1,), (0,)))
            dk = dk + dot(d_scores, queries_t[g], ((1,), (0,)))
            dq_ref[g * HD : (g + 1) * HD, :] += dot(keys, d_scores, ((1,), (0,)))
        dkv_ref[block, 0] = dk.T.astype(BF16)
        dkv_ref[block, 1] = dv.T.astype(BF16)
        return carry

    def blank(block, carry):
        dkv_ref[block] = jnp.zeros(dkv_ref.shape[1:], BF16)
        return carry

    lax.fori_loop(0, own + 1, one, 0)
    lax.fori_loop(own + 1, count, blank, 0)


def attention_specs(tok, count):
    return (
        pl.BlockSpec(memory_space=pltpu.SMEM),
        pl.BlockSpec((GROUPS * HD, tok), lambda b, k: (k, b)),
        pl.BlockSpec((count, 2, HD, tok), lambda b, k: (0, 0, k, b)),
        pl.BlockSpec((1, GROUPS, tok), lambda b, k: (k, 0, b)),
    )


PARAMS = dict(vmem_limit_bytes=48 * 1024 * 1024)


def attend_forward(info, queries, kv, packs, tok, count):
    smem, rows, pairs, stats = attention_specs(tok, count)
    pairs_done = packs * H * tok * tok * count
    return pl.pallas_call(
        functools.partial(forward_kernel, tok),
        grid=(packs, KVH),
        in_specs=[smem, rows, pairs],
        out_specs=[rows, stats],
        out_shape=[
            jax.ShapeDtypeStruct((QW, packs * tok), BF16),
            jax.ShapeDtypeStruct((KVH, GROUPS, packs * tok), F32),
        ],
        scratch_shapes=[pltpu.VMEM((count, tok, tok), F32)],
        compiler_params=pltpu.CompilerParams(**PARAMS),
        cost_estimate=pl.CostEstimate(
            flops=16 * HD * pairs_done, bytes_accessed=10_000_000, transcendentals=pairs_done
        ),
        name="attend_forward",
    )(info, queries, kv)


def attend_backward(info, queries, kv, d_attn, attn, lse, packs, tok, count):
    smem, rows, pairs, stats = attention_specs(tok, count)
    pairs_done = packs * H * tok * tok * count
    return pl.pallas_call(
        functools.partial(backward_kernel, tok, count),
        grid=(packs, KVH),
        in_specs=[smem, rows, pairs, rows, rows, stats],
        out_specs=[rows, pairs],
        out_shape=[
            jax.ShapeDtypeStruct((QW, packs * tok), F32),
            jax.ShapeDtypeStruct((count, 2, KW, packs * tok), BF16),
        ],
        scratch_shapes=[pltpu.VMEM((count, tok, tok), F32)],
        compiler_params=pltpu.CompilerParams(**PARAMS),
        cost_estimate=pl.CostEstimate(
            flops=40 * HD * pairs_done, bytes_accessed=20_000_000, transcendentals=pairs_done
        ),
        name="attend_backward",
    )(info, queries, kv, d_attn, attn, lse)


def rotate(values, cosine, sine):
    tokens = values.shape[-1]
    pairs = values.reshape(-1, 2, HD // 2, tokens)
    first, second = pairs[:, 0], pairs[:, 1]
    return jnp.stack(
        [first * cosine - second * sine, second * cosine + first * sine], 1
    ).reshape(values.shape)


def norm_back(d_normed, values, inverse, gain):
    d_gain = jnp.sum(d_normed * values * inverse, 0)
    scaled = d_normed * gain
    d_values = inverse * scaled - values * (inverse * inverse * inverse) * jnp.mean(
        values * scaled, -1, keepdims=True
    )
    return d_gain, d_values


def local(
    tokens,
    lengths,
    gain_attn,
    w_query,
    w_key,
    w_value,
    w_out,
    gain_ffn,
    w_gate,
    w_up,
    w_down,
    cotangent,
):
    packs, tok, _ = tokens.shape
    rows = packs * tok
    count = lax.axis_size("ctx")
    own = lax.axis_index("ctx")

    gains = lax.all_gather(jnp.stack([gain_attn, gain_ffn]), "dp", axis=1, tiled=True).astype(F32)
    gain_one, gain_two = gains[0], gains[1]
    full_qkv = lax.all_gather(
        jnp.concatenate([w_query, w_key, w_value], 1), "dp", axis=0, tiled=True
    )
    full_out_t = lax.all_gather(w_out.T, "dp", axis=0, tiled=True)
    full_gate_up = lax.all_gather(jnp.concatenate([w_gate, w_up], 1), "dp", axis=0, tiled=True)
    full_down_t = lax.all_gather(w_down.T, "dp", axis=0, tiled=True)

    first_end = lengths[:, 0:1]
    second_end = first_end + lengths[:, 1:2]
    places = own * tok + jnp.arange(tok, dtype=jnp.int32)[None, :]
    begin = jnp.where(places >= second_end, second_end, jnp.where(places >= first_end, first_end, 0))
    positions = (places - begin).reshape(rows).astype(F32)
    half = HD // 2
    frequency = ROPE_BASE ** (-jnp.arange(half, dtype=F32) / half)
    angles = frequency[:, None] * positions[None, :]
    cosine, sine = jnp.cos(angles), jnp.sin(angles)
    info = jnp.concatenate(
        [jnp.full_like(first_end, own), first_end, second_end, jnp.zeros_like(first_end)], 1
    )

    stream = tokens.reshape(rows, D).astype(F32)
    inverse_one = lax.rsqrt(jnp.mean(stream * stream, -1, keepdims=True) + NORM_EPSILON)
    normed = (stream * inverse_one * gain_one).astype(BF16)
    qkv = dot(full_qkv, normed, ((0,), (1,)))
    queries = rotate(qkv[:QW], cosine, sine).astype(BF16) * jnp.asarray(1 / math.sqrt(HD), BF16)
    keys = rotate(qkv[QW : QW + KW], cosine, sine).astype(BF16)
    values = qkv[QW + KW :].astype(BF16)
    kv = lax.all_gather(jnp.stack([keys, values]), "ctx", axis=0, tiled=False)

    attn, lse = attend_forward(info, queries, kv, packs, tok, count)

    middle = stream + dot(attn, full_out_t, ((0,), (1,)))
    inverse_two = lax.rsqrt(jnp.mean(middle * middle, -1, keepdims=True) + NORM_EPSILON)
    normed_two = (middle * inverse_two * gain_two).astype(BF16)
    gate_up = dot(normed_two, full_gate_up, ((1,), (0,)))
    gate, up = gate_up[:, :FF], gate_up[:, FF:]
    sigma = jax.nn.sigmoid(gate)
    silu = gate * sigma
    hidden = (silu * up).astype(BF16)

    cot = cotangent.reshape(rows, D)
    d_hidden = dot(cot, full_down_t, ((1,), (0,)))
    d_gate = (d_hidden * up * sigma * (1.0 + gate * (1.0 - sigma))).astype(BF16)
    d_up = (d_hidden * silu).astype(BF16)

    def reduced(term):
        part = lax.psum_scatter(term, "dp", scatter_dimension=0, tiled=True)
        return lax.psum(part, "ctx").astype(F32)

    g_down = reduced(dot(cot, hidden, ((0,), (0,))).astype(BF16))
    g_gate = reduced(dot(normed_two, d_gate, ((0,), (0,))).astype(BF16))
    g_up = reduced(dot(normed_two, d_up, ((0,), (0,))).astype(BF16))

    output = (middle + dot(hidden, full_down_t, ((1,), (1,)))).astype(BF16)

    d_normed_two = dot(d_gate, full_gate_up[:, :FF], ((1,), (1,))) + dot(
        d_up, full_gate_up[:, FF:], ((1,), (1,))
    )
    d_gain_two, d_middle_norm = norm_back(d_normed_two, middle, inverse_two, gain_two)
    d_middle = cot.astype(F32) + d_middle_norm
    d_mixed = d_middle.astype(BF16)
    d_attn = dot(full_out_t, d_mixed, ((0,), (1,))).astype(BF16)

    dq, dkv_terms = attend_backward(info, queries, kv, d_attn, attn, lse, packs, tok, count)
    g_out = reduced(dot(d_mixed, attn, ((0,), (1,))).astype(BF16))
    dkv = lax.psum_scatter(dkv_terms, "ctx", scatter_dimension=0, tiled=False)

    d_query = rotate(dq * (1 / math.sqrt(HD)), cosine, -sine).astype(BF16)
    d_key = rotate(dkv[0].astype(F32), cosine, -sine).astype(BF16)
    d_qkv = jnp.concatenate([d_query, d_key, dkv[1]], 0)
    g_qkv = reduced(dot(normed, d_qkv, ((0,), (1,))).astype(BF16))
    d_normed = dot(d_qkv, full_qkv, ((0,), (1,)))
    d_gain_one, d_stream = norm_back(d_normed, stream, inverse_one, gain_one)
    d_tokens = (d_middle + d_stream).astype(BF16)

    d_gains = lax.psum(jnp.stack([d_gain_one, d_gain_two]), ("dp", "ctx"))
    width = gain_attn.shape[0]
    share = lax.dynamic_slice_in_dim(d_gains, lax.axis_index("dp") * width, width, 1)

    return (
        output.reshape(packs, tok, D),
        d_tokens.reshape(packs, tok, D),
        share[0],
        g_qkv[:, :QW],
        g_qkv[:, QW : QW + KW],
        g_qkv[:, QW + KW :],
        g_out.T,
        share[1],
        g_gate,
        g_up,
        g_down.T,
    )


def solution(mesh):
    return jax.shard_map(
        local,
        mesh=mesh,
        in_specs=(
            P("dp", "ctx", None),
            P("dp", None),
            P("dp"),
            P("dp", None),
            P("dp", None),
            P("dp", None),
            P(None, "dp"),
            P("dp"),
            P("dp", None),
            P("dp", None),
            P(None, "dp"),
            P("dp", "ctx", None),
        ),
        out_specs=(
            P("dp", "ctx", None),
            P("dp", "ctx", None),
            P("dp"),
            P("dp", None),
            P("dp", None),
            P("dp", None),
            P(None, "dp"),
            P("dp"),
            P("dp", None),
            P("dp", None),
            P(None, "dp"),
        ),
        check_vma=False,
    )
```

```python
import functools
import math

import jax
import jax.numpy as jnp
from jax import lax
from jax.experimental import pallas as pl
from jax.experimental.pallas import tpu as pltpu
from jax.sharding import PartitionSpec as P

D = 960
H = 15
KVH = 5
HD = 64
FF = 2560
GROUPS = H // KVH
QW = H * HD
KW = KVH * HD

NORM_EPSILON = 1e-05
ROPE_BASE = 10000.0
MASKED_SCORE = -1e30
F32 = jnp.float32
BF16 = jnp.bfloat16


def dot(left, right, dims):
    return lax.dot_general(left, right, (dims, ((), ())), preferred_element_type=F32)


def fill_bias(info_ref, bias, tok):
    pack = pl.program_id(0)
    own = info_ref[pack, 0]
    first_end = info_ref[pack, 1]
    second_end = info_ref[pack, 2]
    query = own * tok + lax.broadcasted_iota(jnp.int32, (tok, tok), 1)
    start = jnp.where(
        query >= second_end, second_end, jnp.where(query >= first_end, first_end, 0)
    )

    def one(slot, carry):
        key = (own - slot) * tok + lax.broadcasted_iota(jnp.int32, (tok, tok), 0)
        allowed = (key >= start) & (key <= query)
        bias[slot] = jnp.where(allowed, 0.0, MASKED_SCORE)
        return carry

    lax.fori_loop(0, own + 1, one, 0)


def forward_kernel(tok, info_ref, q_ref, kv_ref, attn_ref, lse_ref, bias):
    own = info_ref[pl.program_id(0), 0]

    @pl.when(pl.program_id(1) == 0)
    def _():
        fill_bias(info_ref, bias, tok)

    def one(block, carry):
        keys = kv_ref[block, 0].T
        values = kv_ref[block, 1]
        mask = bias[block]
        state = []
        for g in range(GROUPS):
            top, total, accum = carry[g]
            scores = dot(keys, q_ref[g * HD : (g + 1) * HD, :], ((1,), (0,))) + mask
            new_top = jnp.maximum(top, jnp.max(scores, 0, keepdims=True))
            scaled = jnp.exp(top - new_top)
            expos = jnp.exp(scores - new_top)
            total = total * scaled + jnp.sum(expos, 0, keepdims=True)
            accum = accum * scaled + dot(values, expos.astype(BF16), ((1,), (0,)))
            state.append((new_top, total, accum))
        return tuple(state)

    begin = tuple(
        (
            jnp.full((1, tok), MASKED_SCORE, F32),
            jnp.zeros((1, tok), F32),
            jnp.zeros((HD, tok), F32),
        )
        for _ in range(GROUPS)
    )
    final = lax.fori_loop(0, own + 1, one, begin)
    for g in range(GROUPS):
        top, total, accum = final[g]
        attn_ref[g * HD : (g + 1) * HD, :] = (accum / total).astype(BF16)
        lse_ref[0, g : g + 1, :] = top + jnp.log(total)


def backward_kernel(
    tok, count, info_ref, q_ref, kv_ref, do_ref, attn_ref, lse_ref, dq_ref, dkv_ref, bias
):
    own = info_ref[pl.program_id(0), 0]

    @pl.when(pl.program_id(1) == 0)
    def _():
        fill_bias(info_ref, bias, tok)

    dq_ref[...] = jnp.zeros_like(dq_ref)
    queries = [q_ref[g * HD : (g + 1) * HD, :] for g in range(GROUPS)]
    d_attn = [do_ref[g * HD : (g + 1) * HD, :] for g in range(GROUPS)]
    queries_t = [value.T for value in queries]
    d_attn_t = [value.T for value in d_attn]
    delta = [
        jnp.sum(
            d_attn[g].astype(F32) * attn_ref[g * HD : (g + 1) * HD, :].astype(F32),
            0,
            keepdims=True,
        )
        for g in range(GROUPS)
    ]

    def one(block, carry):
        keys = kv_ref[block, 0]
        keys_t = keys.T
        values_t = kv_ref[block, 1].T
        mask = bias[block]
        dk = jnp.zeros((tok, HD), F32)
        dv = jnp.zeros((tok, HD), F32)
        for g in range(GROUPS):
            scores = dot(keys_t, queries[g], ((1,), (0,))) + mask
            probs = jnp.exp(scores - lse_ref[0, g : g + 1, :])
            d_probs = dot(values_t, d_attn[g], ((1,), (0,)))
            d_scores = (probs * (d_probs - delta[g])).astype(BF16)
            dv = dv + dot(probs.astype(BF16), d_attn_t[g], ((1,), (0,)))
            dk = dk + dot(d_scores, queries_t[g], ((1,), (0,)))
            dq_ref[g * HD : (g + 1) * HD, :] += dot(keys, d_scores, ((1,), (0,)))
        dkv_ref[block, 0] = dk.T.astype(BF16)
        dkv_ref[block, 1] = dv.T.astype(BF16)
        return carry

    def blank(block, carry):
        dkv_ref[block] = jnp.zeros(dkv_ref.shape[1:], BF16)
        return carry

    lax.fori_loop(0, own + 1, one, 0)
    lax.fori_loop(own + 1, count, blank, 0)


def attention_specs(tok, count):
    return (
        pl.BlockSpec(memory_space=pltpu.SMEM),
        pl.BlockSpec((GROUPS * HD, tok), lambda b, k: (k, b)),
        pl.BlockSpec((count, 2, HD, tok), lambda b, k: (0, 0, k, b)),
        pl.BlockSpec((1, GROUPS, tok), lambda b, k: (k, 0, b)),
    )


PARAMS = dict(vmem_limit_bytes=48 * 1024 * 1024)


def attend_forward(info, queries, kv, packs, tok, count):
    smem, rows, pairs, stats = attention_specs(tok, count)
    pairs_done = packs * H * tok * tok * count
    return pl.pallas_call(
        functools.partial(forward_kernel, tok),
        grid=(packs, KVH),
        in_specs=[smem, rows, pairs],
        out_specs=[rows, stats],
        out_shape=[
            jax.ShapeDtypeStruct((QW, packs * tok), BF16),
            jax.ShapeDtypeStruct((KVH, GROUPS, packs * tok), F32),
        ],
        scratch_shapes=[pltpu.VMEM((count, tok, tok), F32)],
        compiler_params=pltpu.CompilerParams(**PARAMS),
        cost_estimate=pl.CostEstimate(
            flops=16 * HD * pairs_done, bytes_accessed=10_000_000, transcendentals=pairs_done
        ),
        name="attend_forward",
    )(info, queries, kv)


def attend_backward(info, queries, kv, d_attn, attn, lse, packs, tok, count):
    smem, rows, pairs, stats = attention_specs(tok, count)
    pairs_done = packs * H * tok * tok * count
    return pl.pallas_call(
        functools.partial(backward_kernel, tok, count),
        grid=(packs, KVH),
        in_specs=[smem, rows, pairs, rows, rows, stats],
        out_specs=[rows, pairs],
        out_shape=[
            jax.ShapeDtypeStruct((QW, packs * tok), F32),
            jax.ShapeDtypeStruct((count, 2, KW, packs * tok), BF16),
        ],
        scratch_shapes=[pltpu.VMEM((count, tok, tok), F32)],
        compiler_params=pltpu.CompilerParams(**PARAMS),
        cost_estimate=pl.CostEstimate(
            flops=40 * HD * pairs_done, bytes_accessed=20_000_000, transcendentals=pairs_done
        ),
        name="attend_backward",
    )(info, queries, kv, d_attn, attn, lse)


def rotate(values, cosine, sine):
    tokens = values.shape[-1]
    pairs = values.reshape(-1, 2, HD // 2, tokens)
    first, second = pairs[:, 0], pairs[:, 1]
    return jnp.stack(
        [first * cosine - second * sine, second * cosine + first * sine], 1
    ).reshape(values.shape)


def norm_back(d_normed, values, inverse, gain):
    d_gain = jnp.sum(d_normed * values * inverse, 0)
    scaled = d_normed * gain
    d_values = inverse * scaled - values * (inverse * inverse * inverse) * jnp.mean(
        values * scaled, -1, keepdims=True
    )
    return d_gain, d_values


ORDER = (0, 2, 4, 6, 1, 3, 5, 7)


def swap(value, bit):
    return lax.ppermute(value, "dp", [(i, i ^ bit) for i in range(8)])


def gather_shards(shard):
    middle = shard.shape[0] // 16 * 8
    from_x, from_y = swap(shard, 2), swap(shard, 4)
    diagonal = jnp.concatenate([swap(from_x[:middle], 4), swap(from_y[middle:], 2)], 0)
    near = (shard, from_x, from_y, diagonal)
    return jnp.concatenate(near + tuple(swap(part, 1) for part in near), 0)


def add(left, right):
    return (left.astype(F32) + right.astype(F32)).astype(BF16)


def reduce_shards(keep, send):
    columns = keep.shape[1]
    own = add(keep, swap(send, 1)).reshape(4, -1, columns)
    split = columns // 256 * 128
    one = own[:, :, :split]
    two = own[:, :, split:]
    from_x = swap(jnp.stack([one[1], one[3]]), 2)
    from_y = swap(two[2:], 4)
    last_y = swap(add(one[2], from_x[1]), 4)
    last_x = swap(add(two[1], from_y[1]), 2)
    done_one = add(add(one[0], from_x[0]), last_y)
    done_two = add(add(two[0], from_y[0]), last_x)
    return jnp.concatenate([done_one, done_two], 1)


def local(
    tokens,
    lengths,
    gain_attn,
    w_query,
    w_key,
    w_value,
    w_out,
    gain_ffn,
    w_gate,
    w_up,
    w_down,
    cotangent,
):
    packs, tok, _ = tokens.shape
    rows = packs * tok
    count = lax.axis_size("ctx")
    own = lax.axis_index("ctx")
    direct = lax.axis_size("dp") == 8
    width = D // lax.axis_size("dp")
    half_model = D // 2

    if direct:
        place = jnp.arange(D, dtype=jnp.int32)
        shard = jnp.bitwise_xor(
            jnp.repeat(jnp.asarray(ORDER, jnp.int32), width), lax.axis_index("dp")
        )
        chosen = (place[:, None] == (shard * width + place % width)[None, :]).astype(BF16)

    def arrange(value):
        return dot(value, chosen, ((1,), (0,))).astype(BF16) if direct else value

    def restore(value):
        return dot(value, chosen, ((1,), (1,))).astype(BF16) if direct else value

    def gathered(value):
        if direct:
            return gather_shards(value)
        return lax.all_gather(value, "dp", axis=0, tiled=True)

    full_qkv = gathered(
        jnp.concatenate([w_query, w_key, w_value, gain_attn[:, None], gain_ffn[:, None]], 1)
    )
    down_out = jnp.concatenate([w_down.T, w_out.T], 1)
    gate_up = jnp.concatenate([w_gate, w_up], 1)
    full_qkv, down_out, gate_up = lax.optimization_barrier((full_qkv, down_out, gate_up))
    full_gate_up = gathered(gate_up)
    full_down_out = gathered(down_out)
    full_down_t, full_out_t = full_down_out[:, :FF], full_down_out[:, FF:]
    gains = full_qkv[:, QW + 2 * KW :].astype(F32).T
    gain_one, gain_two = gains[0], gains[1]

    first_end = lengths[:, 0:1]
    second_end = first_end + lengths[:, 1:2]
    places = own * tok + jnp.arange(tok, dtype=jnp.int32)[None, :]
    begin = jnp.where(places >= second_end, second_end, jnp.where(places >= first_end, first_end, 0))
    positions = (places - begin).reshape(rows).astype(F32)
    half = HD // 2
    frequency = ROPE_BASE ** (-jnp.arange(half, dtype=F32) / half)
    angles = frequency[:, None] * positions[None, :]
    cosine, sine = jnp.cos(angles), jnp.sin(angles)
    info = jnp.concatenate(
        [jnp.full_like(first_end, own), first_end, second_end, jnp.zeros_like(first_end)], 1
    )

    stream = arrange(tokens.reshape(rows, D)).astype(F32)
    cot = arrange(cotangent.reshape(rows, D))
    inverse_one = lax.rsqrt(jnp.mean(stream * stream, -1, keepdims=True) + NORM_EPSILON)
    normed = (stream * inverse_one * gain_one).astype(BF16)
    qkv = dot(full_qkv, normed, ((0,), (1,)))
    queries = rotate(qkv[:QW], cosine, sine).astype(BF16) * jnp.asarray(1 / math.sqrt(HD), BF16)
    keys = rotate(qkv[QW : QW + KW], cosine, sine).astype(BF16)
    values = qkv[QW + KW : QW + 2 * KW].astype(BF16)
    own_kv = jnp.stack([keys, values])
    kv = jnp.stack(
        [own_kv]
        + [
            lax.ppermute(own_kv, "ctx", [(i, i + d) for i in range(count - d)])
            for d in range(1, count)
        ]
    )

    attn, lse = attend_forward(info, queries, kv, packs, tok, count)

    middle = stream + dot(attn, full_out_t, ((0,), (1,)))
    inverse_two = lax.rsqrt(jnp.mean(middle * middle, -1, keepdims=True) + NORM_EPSILON)
    normed_two = (middle * inverse_two * gain_two).astype(BF16)
    gate_up = dot(normed_two, full_gate_up, ((1,), (0,)))
    gate, up = gate_up[:, :FF], gate_up[:, FF:]
    sigma = jax.nn.sigmoid(gate)
    silu = gate * sigma
    hidden = (silu * up).astype(BF16)

    d_hidden = dot(cot, full_down_t, ((1,), (0,)))
    d_gate = (d_hidden * up * sigma * (1.0 + gate * (1.0 - sigma))).astype(BF16)
    d_up = (d_hidden * silu).astype(BF16)

    def reduced(left, right, axis, extra=()):
        def term(part, extra_part):
            product = dot(part, right, ((0,), (axis,))).astype(BF16)
            return jnp.concatenate((product,) + extra_part, 1)

        if not direct:
            return lax.psum_scatter(term(left, extra), "dp", scatter_dimension=0, tiled=True)
        send = term(left[:, half_model:], tuple(e[half_model:] for e in extra))
        keep = term(left[:, :half_model], tuple(e[:half_model] for e in extra))
        return reduce_shards(keep, send)

    p_down = reduced(cot, hidden, 0)
    p_gate = reduced(normed_two, d_gate, 0)
    p_up = reduced(normed_two, d_up, 0)

    output = (middle + dot(hidden, full_down_t, ((1,), (1,)))).astype(BF16)

    d_normed_two = dot(d_gate, full_gate_up[:, :FF], ((1,), (1,))) + dot(
        d_up, full_gate_up[:, FF:], ((1,), (1,))
    )
    d_gain_two, d_middle_norm = norm_back(d_normed_two, middle, inverse_two, gain_two)
    d_middle = cot.astype(F32) + d_middle_norm
    d_mixed = d_middle.astype(BF16)
    d_attn = dot(full_out_t, d_mixed, ((0,), (1,))).astype(BF16)

    dq, dkv_terms = attend_backward(info, queries, kv, d_attn, attn, lse, packs, tok, count)
    p_out = reduced(d_mixed, attn, 1)
    dkv = dkv_terms[0].astype(F32)
    for d in range(1, count):
        moved = lax.ppermute(dkv_terms[d], "ctx", [(i + d, i) for i in range(count - d)])
        dkv = dkv + moved.astype(F32)

    d_query = rotate(dq * (1 / math.sqrt(HD)), cosine, -sine).astype(BF16)
    d_key = rotate(dkv[0], cosine, -sine).astype(BF16)
    d_qkv = jnp.concatenate([d_query, d_key, dkv[1].astype(BF16)], 0)
    d_normed = dot(
        jnp.concatenate([d_qkv, jnp.zeros((2, rows), BF16)], 0), full_qkv, ((0,), (1,))
    )
    d_gain_one, d_stream = norm_back(d_normed, stream, inverse_one, gain_one)
    p_qkv = reduced(
        normed, d_qkv, 1, (d_gain_one.astype(BF16)[:, None], d_gain_two.astype(BF16)[:, None])
    )
    d_tokens = restore((d_middle + d_stream).astype(BF16))

    early = lax.psum((p_down, p_gate, p_up), "ctx")
    early, p_out, p_qkv = lax.optimization_barrier((early, p_out, p_qkv))
    late = lax.psum((p_out, p_qkv), "ctx")
    g_down, g_gate, g_up = (value.astype(F32) for value in early)
    g_out, g_qkv = (value.astype(F32) for value in late)

    return (
        restore(output).reshape(packs, tok, D),
        d_tokens.reshape(packs, tok, D),
        g_qkv[:, QW + 2 * KW],
        g_qkv[:, :QW],
        g_qkv[:, QW : QW + KW],
        g_qkv[:, QW + KW : QW + 2 * KW],
        g_out.T,
        g_qkv[:, QW + 2 * KW + 1],
        g_gate,
        g_up,
        g_down.T,
    )


def solution(mesh):
    return jax.shard_map(
        local,
        mesh=mesh,
        in_specs=(
            P("dp", "ctx", None),
            P("dp", None),
            P("dp"),
            P("dp", None),
            P("dp", None),
            P("dp", None),
            P(None, "dp"),
            P("dp"),
            P("dp", None),
            P("dp", None),
            P(None, "dp"),
            P("dp", "ctx", None),
        ),
        out_specs=(
            P("dp", "ctx", None),
            P("dp", "ctx", None),
            P("dp"),
            P("dp", None),
            P("dp", None),
            P("dp", None),
            P(None, "dp"),
            P("dp"),
            P("dp", None),
            P("dp", None),
            P(None, "dp"),
        ),
        check_vma=False,
    )
```

```python
import functools
import math

import jax
import jax.numpy as jnp
from jax import lax
from jax.experimental import pallas as pl
from jax.experimental.pallas import tpu as pltpu
from jax.sharding import PartitionSpec as P

D = 960
H = 15
KVH = 5
HD = 64
FF = 2560
GROUPS = H // KVH
QW = H * HD
KW = KVH * HD

NORM_EPSILON = 1e-05
ROPE_BASE = 10000.0
MASKED_SCORE = -1e30
F32 = jnp.float32
BF16 = jnp.bfloat16


def dot(left, right, dims):
    return lax.dot_general(left, right, (dims, ((), ())), preferred_element_type=F32)


def fill_bias(info_ref, bias, tok):
    own = info_ref[0, 0]
    first_end = info_ref[0, 1]
    second_end = info_ref[0, 2]
    query = own * tok + lax.broadcasted_iota(jnp.int32, (tok, tok), 1)
    start = jnp.where(
        query >= second_end, second_end, jnp.where(query >= first_end, first_end, 0)
    )

    def one(slot, carry):
        key = (own - slot) * tok + lax.broadcasted_iota(jnp.int32, (tok, tok), 0)
        allowed = (key >= start) & (key <= query)
        bias[slot] = jnp.where(allowed, 0.0, MASKED_SCORE)
        return carry

    lax.fori_loop(0, own + 1, one, 0)


def forward_kernel(tok, info_ref, q_ref, kv_ref, attn_ref, lse_ref, bias):
    own = info_ref[0, 0]

    @pl.when(pl.program_id(0) == 0)
    def _():
        fill_bias(info_ref, bias, tok)

    def one(block, carry):
        keys = kv_ref[block, 0].T
        values = kv_ref[block, 1]
        mask = bias[block]
        state = []
        for g in range(GROUPS):
            top, total, accum = carry[g]
            scores = dot(keys, q_ref[g * HD : (g + 1) * HD, :], ((1,), (0,))) + mask
            new_top = jnp.maximum(top, jnp.max(scores, 0, keepdims=True))
            scaled = jnp.exp(top - new_top)
            expos = jnp.exp(scores - new_top)
            total = total * scaled + jnp.sum(expos, 0, keepdims=True)
            accum = accum * scaled + dot(values, expos.astype(BF16), ((1,), (0,)))
            state.append((new_top, total, accum))
        return tuple(state)

    begin = tuple(
        (
            jnp.full((1, tok), MASKED_SCORE, F32),
            jnp.zeros((1, tok), F32),
            jnp.zeros((HD, tok), F32),
        )
        for _ in range(GROUPS)
    )
    final = lax.fori_loop(0, own + 1, one, begin)
    for g in range(GROUPS):
        top, total, accum = final[g]
        attn_ref[g * HD : (g + 1) * HD, :] = (accum / total).astype(BF16)
        lse_ref[0, g : g + 1, :] = top + jnp.log(total)


def backward_kernel(
    tok, count, info_ref, q_ref, kv_ref, do_ref, attn_ref, lse_ref, dq_ref, dkv_ref, bias
):
    own = info_ref[0, 0]

    @pl.when(pl.program_id(0) == 0)
    def _():
        fill_bias(info_ref, bias, tok)

    dq_ref[...] = jnp.zeros_like(dq_ref)
    queries = [q_ref[g * HD : (g + 1) * HD, :] for g in range(GROUPS)]
    d_attn = [do_ref[g * HD : (g + 1) * HD, :] for g in range(GROUPS)]
    queries_t = [value.T for value in queries]
    d_attn_t = [value.T for value in d_attn]
    delta = [
        jnp.sum(
            d_attn[g].astype(F32) * attn_ref[g * HD : (g + 1) * HD, :].astype(F32),
            0,
            keepdims=True,
        )
        for g in range(GROUPS)
    ]

    def one(block, carry):
        keys = kv_ref[block, 0]
        keys_t = keys.T
        values_t = kv_ref[block, 1].T
        mask = bias[block]
        dk = jnp.zeros((tok, HD), F32)
        dv = jnp.zeros((tok, HD), F32)
        for g in range(GROUPS):
            scores = dot(keys_t, queries[g], ((1,), (0,))) + mask
            probs = jnp.exp(scores - lse_ref[0, g : g + 1, :])
            d_probs = dot(values_t, d_attn[g], ((1,), (0,)))
            d_scores = (probs * (d_probs - delta[g])).astype(BF16)
            dv = dv + dot(probs.astype(BF16), d_attn_t[g], ((1,), (0,)))
            dk = dk + dot(d_scores, queries_t[g], ((1,), (0,)))
            dq_ref[g * HD : (g + 1) * HD, :] += dot(keys, d_scores, ((1,), (0,)))
        dkv_ref[block, 0] = dk.T.astype(BF16)
        dkv_ref[block, 1] = dv.T.astype(BF16)
        return carry

    def blank(block, carry):
        dkv_ref[block] = jnp.zeros(dkv_ref.shape[1:], BF16)
        return carry

    lax.fori_loop(0, own + 1, one, 0)
    lax.fori_loop(own + 1, count, blank, 0)


def attention_specs(pack, tok, count):
    return (
        pl.BlockSpec(memory_space=pltpu.SMEM),
        pl.BlockSpec((GROUPS * HD, tok), lambda k: (k, pack)),
        pl.BlockSpec((GROUPS * HD, tok), lambda k: (k, 0)),
        pl.BlockSpec((count, 2, HD, tok), lambda k: (0, 0, k, 0)),
        pl.BlockSpec((1, GROUPS, tok), lambda k: (k, 0, 0)),
    )


PARAMS = dict(vmem_limit_bytes=48 * 1024 * 1024)


def with_awaited(kernel, operands, awaited):
    def body(*refs):
        kernel(*refs[:operands], *refs[operands + awaited :])

    return body


def attend_forward(pack, info, queries, kv, awaited, tok, count):
    smem, columns, rows, pairs, stats = attention_specs(pack, tok, count)
    pairs_done = H * tok * tok * count
    return pl.pallas_call(
        with_awaited(functools.partial(forward_kernel, tok), 3, len(awaited)),
        grid=(KVH,),
        in_specs=[smem, columns, pairs] + [pl.BlockSpec(memory_space=pl.ANY)] * len(awaited),
        out_specs=[rows, stats],
        out_shape=[
            jax.ShapeDtypeStruct((QW, tok), BF16),
            jax.ShapeDtypeStruct((KVH, GROUPS, tok), F32),
        ],
        scratch_shapes=[pltpu.VMEM((count, tok, tok), F32)],
        compiler_params=pltpu.CompilerParams(**PARAMS),
        cost_estimate=pl.CostEstimate(
            flops=16 * HD * pairs_done, bytes_accessed=5_000_000, transcendentals=pairs_done
        ),
        name="attend_forward",
    )(info, queries, kv, *awaited)


def attend_backward(pack, info, queries, kv, d_attn, attn, lse, awaited, tok, count):
    smem, columns, rows, pairs, stats = attention_specs(pack, tok, count)
    pairs_done = H * tok * tok * count
    return pl.pallas_call(
        with_awaited(functools.partial(backward_kernel, tok, count), 6, len(awaited)),
        grid=(KVH,),
        in_specs=[smem, columns, pairs, columns, rows, stats]
        + [pl.BlockSpec(memory_space=pl.ANY)] * len(awaited),
        out_specs=[rows, pairs],
        out_shape=[
            jax.ShapeDtypeStruct((QW, tok), F32),
            jax.ShapeDtypeStruct((count, 2, KW, tok), BF16),
        ],
        scratch_shapes=[pltpu.VMEM((count, tok, tok), F32)],
        compiler_params=pltpu.CompilerParams(**PARAMS),
        cost_estimate=pl.CostEstimate(
            flops=40 * HD * pairs_done, bytes_accessed=10_000_000, transcendentals=pairs_done
        ),
        name="attend_backward",
    )(info, queries, kv, d_attn, attn, lse, *awaited)


def rotate(values, cosine, sine):
    tokens = values.shape[-1]
    pairs = values.reshape(-1, 2, HD // 2, tokens)
    first, second = pairs[:, 0], pairs[:, 1]
    return jnp.stack(
        [first * cosine - second * sine, second * cosine + first * sine], 1
    ).reshape(values.shape)


def norm_back(d_normed, values, inverse, gain):
    d_gain = jnp.sum(d_normed * values * inverse, 0)
    scaled = d_normed * gain
    d_values = inverse * scaled - values * (inverse * inverse * inverse) * jnp.mean(
        values * scaled, -1, keepdims=True
    )
    return d_gain, d_values


ORDER = (0, 2, 4, 6, 1, 3, 5, 7)


def swap(value, bit):
    return lax.ppermute(value, "dp", [(i, i ^ bit) for i in range(8)])


def gather_near(shard):
    return shard, swap(shard, 2), swap(shard, 4)


def gather_rest(shard, from_x, from_y):
    middle = shard.shape[0] // 16 * 8
    diagonal = jnp.concatenate([swap(from_x[:middle], 4), swap(from_y[middle:], 2)], 0)
    near = (shard, from_x, from_y, diagonal)
    return jnp.concatenate(near + tuple(swap(part, 1) for part in near), 0)


def add(left, right):
    return (left.astype(F32) + right.astype(F32)).astype(BF16)


def reduce_cores(keep, send):
    return add(keep, swap(send, 1)).reshape(4, -1, keep.shape[1])


def reduce_chips(own):
    split = own.shape[2] // 256 * 128
    one = own[:, :, :split]
    two = own[:, :, split:]
    from_x = swap(jnp.stack([one[1], one[3]]), 2)
    from_y = swap(two[2:], 4)
    last_y = swap(add(one[2], from_x[1]), 4)
    last_x = swap(add(two[1], from_y[1]), 2)
    done_one = add(add(one[0], from_x[0]), last_y)
    done_two = add(add(two[0], from_y[0]), last_x)
    return jnp.concatenate([done_one, done_two], 1)


def sum_over_ctx(value, count):
    if count & (count - 1):
        return lax.psum(value, "ctx")
    step = 1
    while step < count:
        moved = lax.ppermute(value, "ctx", [(i, i ^ step) for i in range(count)])
        value = add(value, moved)
        step *= 2
    return value


def local(
    tokens,
    lengths,
    gain_attn,
    w_query,
    w_key,
    w_value,
    w_out,
    gain_ffn,
    w_gate,
    w_up,
    w_down,
    cotangent,
):
    packs, tok, _ = tokens.shape
    rows = packs * tok
    count = lax.axis_size("ctx")
    own = lax.axis_index("ctx")
    direct = lax.axis_size("dp") == 8
    width = D // lax.axis_size("dp")
    half_model = D // 2

    if direct:
        place = jnp.arange(D, dtype=jnp.int32)
        shard = jnp.bitwise_xor(
            jnp.repeat(jnp.asarray(ORDER, jnp.int32), width), lax.axis_index("dp")
        )
        chosen = (place[:, None] == (shard * width + place % width)[None, :]).astype(BF16)

    def arrange(value):
        return dot(value, chosen, ((1,), (0,))).astype(BF16) if direct else value

    def restore(value):
        return dot(value, chosen, ((1,), (1,))).astype(BF16) if direct else value

    def gather_begin(value):
        return gather_near(value) if direct else (value,)

    def gather_end(parts):
        if direct:
            return gather_rest(*parts)
        return lax.all_gather(parts[0], "dp", axis=0, tiled=True)

    full_qkv = gather_end(
        gather_begin(
            jnp.concatenate([w_query, w_key, w_value, gain_attn[:, None], gain_ffn[:, None]], 1)
        )
    )
    down_out = jnp.concatenate([w_down.T, w_out.T], 1)
    gate_up = jnp.concatenate([w_gate, w_up], 1)
    full_qkv, down_out, gate_up = lax.optimization_barrier((full_qkv, down_out, gate_up))
    near_down_out = gather_begin(down_out)
    near_gate_up = gather_begin(gate_up)
    full_down_out = gather_end(near_down_out)
    full_gate_up = gather_end(near_gate_up)
    full_down_t, full_out_t = full_down_out[:, :FF], full_down_out[:, FF:]
    gains = full_qkv[:, QW + 2 * KW :].astype(F32).T
    gain_one, gain_two = gains[0], gains[1]

    first_end = lengths[:, 0:1]
    second_end = first_end + lengths[:, 1:2]
    places = own * tok + jnp.arange(tok, dtype=jnp.int32)[None, :]
    begin = jnp.where(places >= second_end, second_end, jnp.where(places >= first_end, first_end, 0))
    positions = (places - begin).reshape(rows).astype(F32)
    half = HD // 2
    frequency = ROPE_BASE ** (-jnp.arange(half, dtype=F32) / half)
    angles = frequency[:, None] * positions[None, :]
    cosine, sine = jnp.cos(angles), jnp.sin(angles)
    info = jnp.concatenate(
        [jnp.full_like(first_end, own), first_end, second_end, jnp.zeros_like(first_end)], 1
    )

    stream = arrange(tokens.reshape(rows, D)).astype(F32)
    cot = arrange(cotangent.reshape(rows, D))
    inverse_one = lax.rsqrt(jnp.mean(stream * stream, -1, keepdims=True) + NORM_EPSILON)
    normed = (stream * inverse_one * gain_one).astype(BF16)
    qkv = dot(full_qkv, normed, ((0,), (1,)))
    queries = rotate(qkv[:QW], cosine, sine).astype(BF16) * jnp.asarray(1 / math.sqrt(HD), BF16)
    keys = rotate(qkv[QW : QW + KW], cosine, sine).astype(BF16)
    values = qkv[QW + KW : QW + 2 * KW].astype(BF16)
    own_kv = jnp.stack([keys, values])

    def spread(block):
        return jnp.stack(
            [block]
            + [
                lax.ppermute(block, "ctx", [(i, i + d) for i in range(count - d)])
                for d in range(1, count)
            ]
        )

    kv = [spread(own_kv[:, :, b * tok : (b + 1) * tok]) for b in range(packs)]
    attn_parts, lse = [], []
    for b in range(packs):
        awaited = near_down_out[1:] + near_gate_up[1:] if b == packs - 1 else ()
        attn_part, lse_part = attend_forward(
            b, info[b : b + 1], queries, kv[b], awaited, tok, count
        )
        attn_parts.append(attn_part)
        lse.append(lse_part)
    attn = jnp.concatenate(attn_parts, 1)

    middle = stream + dot(attn, full_out_t, ((0,), (1,)))
    inverse_two = lax.rsqrt(jnp.mean(middle * middle, -1, keepdims=True) + NORM_EPSILON)
    normed_two = (middle * inverse_two * gain_two).astype(BF16)
    gate_up = dot(normed_two, full_gate_up, ((1,), (0,)))
    gate, up = gate_up[:, :FF], gate_up[:, FF:]
    sigma = jax.nn.sigmoid(gate)
    silu = gate * sigma
    hidden = (silu * up).astype(BF16)

    d_hidden = dot(cot, full_down_t, ((1,), (0,)))
    d_gate = (d_hidden * up * sigma * (1.0 + gate * (1.0 - sigma))).astype(BF16)
    d_up = (d_hidden * silu).astype(BF16)

    def reduce_begin(left, right, axis, extra=()):
        def term(part, extra_part):
            product = dot(part, right, ((0,), (axis,))).astype(BF16)
            return jnp.concatenate((product,) + extra_part, 1)

        if not direct:
            return term(left, extra)
        send = term(left[:, half_model:], tuple(e[half_model:] for e in extra))
        keep = term(left[:, :half_model], tuple(e[:half_model] for e in extra))
        return reduce_cores(keep, send)

    def reduce_end(value):
        if direct:
            return reduce_chips(value)
        return lax.psum_scatter(value, "dp", scatter_dimension=0, tiled=True)

    begun = [
        reduce_begin(cot, hidden, 0),
        reduce_begin(normed_two, d_gate, 0),
        reduce_begin(normed_two, d_up, 0),
    ]

    output = (middle + dot(hidden, full_down_t, ((1,), (1,)))).astype(BF16)

    d_normed_two = dot(d_gate, full_gate_up[:, :FF], ((1,), (1,))) + dot(
        d_up, full_gate_up[:, FF:], ((1,), (1,))
    )
    d_gain_two, d_middle_norm = norm_back(d_normed_two, middle, inverse_two, gain_two)
    d_middle = cot.astype(F32) + d_middle_norm
    d_mixed = d_middle.astype(BF16)
    d_attn = dot(full_out_t, d_mixed, ((0,), (1,))).astype(BF16)

    begun.append(reduce_begin(d_mixed, attn, 1))
    dq_parts, dkv_parts = [], []
    for b in range(packs):
        awaited = tuple(begun) if b == packs - 1 else ()
        dq_part, terms = attend_backward(
            b, info[b : b + 1], queries, kv[b], d_attn, attn_parts[b], lse[b], awaited, tok, count
        )
        dkv_part = terms[0].astype(F32)
        for d in range(1, count):
            moved = lax.ppermute(terms[d], "ctx", [(i + d, i) for i in range(count - d)])
            dkv_part = dkv_part + moved.astype(F32)
        dq_parts.append(dq_part)
        dkv_parts.append(dkv_part)
    dq = jnp.concatenate(dq_parts, 1)
    dkv = jnp.concatenate(dkv_parts, 2)
    early = lax.psum(tuple(reduce_end(value) for value in begun), "ctx")

    d_query = rotate(dq * (1 / math.sqrt(HD)), cosine, -sine).astype(BF16)
    d_key = rotate(dkv[0], cosine, -sine).astype(BF16)
    d_qkv = jnp.concatenate([d_query, d_key, dkv[1].astype(BF16)], 0)
    d_normed = dot(
        jnp.concatenate([d_qkv, jnp.zeros((2, rows), BF16)], 0), full_qkv, ((0,), (1,))
    )
    d_gain_one, d_stream = norm_back(d_normed, stream, inverse_one, gain_one)
    p_qkv = reduce_end(
        reduce_begin(
            normed, d_qkv, 1, (d_gain_one.astype(BF16)[:, None], d_gain_two.astype(BF16)[:, None])
        )
    )
    d_tokens = restore((d_middle + d_stream).astype(BF16))

    g_down, g_gate, g_up, g_out = (value.astype(F32) for value in early)
    g_qkv = sum_over_ctx(p_qkv, count).astype(F32)

    return (
        restore(output).reshape(packs, tok, D),
        d_tokens.reshape(packs, tok, D),
        g_qkv[:, QW + 2 * KW],
        g_qkv[:, :QW],
        g_qkv[:, QW : QW + KW],
        g_qkv[:, QW + KW : QW + 2 * KW],
        g_out.T,
        g_qkv[:, QW + 2 * KW + 1],
        g_gate,
        g_up,
        g_down.T,
    )


def solution(mesh):
    return jax.shard_map(
        local,
        mesh=mesh,
        in_specs=(
            P("dp", "ctx", None),
            P("dp", None),
            P("dp"),
            P("dp", None),
            P("dp", None),
            P("dp", None),
            P(None, "dp"),
            P("dp"),
            P("dp", None),
            P("dp", None),
            P(None, "dp"),
            P("dp", "ctx", None),
        ),
        out_specs=(
            P("dp", "ctx", None),
            P("dp", "ctx", None),
            P("dp"),
            P("dp", None),
            P("dp", None),
            P("dp", None),
            P(None, "dp"),
            P("dp"),
            P("dp", None),
            P("dp", None),
            P(None, "dp"),
        ),
        check_vma=False,
    )
```
